512 devices in a mesh: grp: 4 (over z_hi, core), seq: 128 (over x, y, z_lo).
Axes of the slice: x: 4, y: 4, z: 16 (z_hi: 2, z_lo: 8; z = z_hi * 8 + z_lo), core: 2. Of those that a mesh axis runs over, the one named last changes fastest.
Arguments:
- cand_queries: bfloat16 [4096, 128, 128], P(('grp', 'seq')), may hold values from -256 to 256
- candidate_keys: bfloat16 [512, 128, 128], P(('grp', 'seq')), may hold values from -6 to 6
- candidate_values: bfloat16 [512, 128, 128], P(('grp', 'seq')), may hold values from -24 to 24
- prefix_rotated_keys: bfloat16 [2048, 1024], P(('grp', 'seq')), may hold values from -6.1 to 6.1
- prefix_value_matrix: bfloat16 [2048, 1024], P(('grp', 'seq')), may hold values from -24 to 24
- lengths: int32 [64], replicated, may hold values from 32 to 128
Outputs:
- attended: bfloat16 [4096, 128, 128], P(('grp', 'seq'))
The draws below stay inside these ranges and needn't reach their ends.
All inputs are finite; a program needn't handle non-finite values.
Results may differ from the reference program's by a relative error of at most 0.0076.
Values may be sent and summed in bfloat16 or wider, within the bound.
A program may use at most 64 MiB of HBM per device.

```python
import math
import jax
import jax.numpy as jnp
from jax import lax

QUERY_HEADS = 64
KEY_VALUE_HEADS = 8
HEAD_WIDTH = 128
CANDIDATE_SLOTS = 128
CANDIDATE_TOTAL = 64
PREFIX_TOKENS = 2048


def prefix_anchor(key):
    drawn_row_list = jax.random.normal(jax.random.fold_in(key, 11), (PREFIX_TOKENS, KEY_VALUE_HEADS, HEAD_WIDTH), jnp.float32)
    return jnp.clip(drawn_row_list, -6.0, 6.0)


def draw_prefix_rotated_keys(key, part):
    anchor_row_list = prefix_anchor(key)
    return anchor_row_list.reshape(PREFIX_TOKENS, KEY_VALUE_HEADS * HEAD_WIDTH).astype(jnp.bfloat16)


def draw_cand_queries(key, part):

    def one_candidate(index):
        own_key = jax.random.fold_in(key, 100 + index)
        noise = 2.0 * jax.random.normal(jax.random.fold_in(own_key, 21), (QUERY_HEADS, CANDIDATE_SLOTS, HEAD_WIDTH), jnp.float32)
        noise = jnp.clip(noise, -12.0, 12.0)
        return noise
    rows = lax.map(one_candidate, jnp.arange(CANDIDATE_TOTAL))
    return rows.reshape(CANDIDATE_TOTAL * QUERY_HEADS, CANDIDATE_SLOTS, HEAD_WIDTH).astype(jnp.bfloat16)


def place_ends(entries, stream_key, least, high):
    longest = entries.shape.index(max(entries.shape))
    spots = []
    for shift in (0, 1):
        where = [jax.random.randint(jax.random.fold_in(stream_key, axis), (), 0, length) for axis, length in enumerate(entries.shape)]
        where[longest] = (where[longest] + shift) % entries.shape[longest]
        spots.append(tuple(where))
    return entries.at[spots[0]].set(least).at[spots[1]].set(high)


def block_scale(key, dims, pieces, low, high):
    level = 1.0
    for position, shards_of in pieces:
        draws = jax.random.uniform(jax.random.fold_in(jax.random.fold_in(key, 6), position), (shards_of,), jnp.float32, low / len(pieces), high / len(pieces))
        level = level * jnp.repeat(jnp.exp(draws), dims[position] // shards_of).reshape((-1,) + (1,) * (len(dims) - 1 - position))
    return level


def scatter_about(key, extent, deviation, most, cuts=(), held_as=jnp.bfloat16):
    values = deviation * jax.random.normal(key, extent, jnp.float32)
    if cuts:
        values = values * block_scale(key, extent, cuts, -0.22, 0.18)
    return jnp.clip(values, -most, most).astype(held_as)


def setup_inputs(seed: int = 0) -> dict:
    key_of = jax.random.split(jax.random.key(seed), 7)
    return {
        "cand_queries": draw_cand_queries(jax.random.fold_in(key_of[6], 71), 0),
        "candidate_keys": scatter_about(key_of[1], (CANDIDATE_TOTAL * KEY_VALUE_HEADS, CANDIDATE_SLOTS, HEAD_WIDTH), 1.0, 6.0, ((0, 512),)),
        "candidate_values": scatter_about(key_of[2], (CANDIDATE_TOTAL * KEY_VALUE_HEADS, CANDIDATE_SLOTS, HEAD_WIDTH), 4.0, 24.0, ((0, 512),)),
        "prefix_rotated_keys": draw_prefix_rotated_keys(jax.random.fold_in(key_of[6], 71), 0),
        "prefix_value_matrix": scatter_about(key_of[4], (PREFIX_TOKENS, KEY_VALUE_HEADS * HEAD_WIDTH), 4.0, 24.0, ((0, 512),)),
        "lengths": place_ends(jax.random.randint(key_of[5], (CANDIDATE_TOTAL,), CANDIDATE_SLOTS // 4, CANDIDATE_SLOTS + 1), jax.random.fold_in(key_of[5], 1), CANDIDATE_SLOTS // 4, CANDIDATE_SLOTS).astype(jnp.int32),
    }


rope_base = 500000.0

def rotate(vectors, positions):
    half_width = vectors.shape[-1] // 2
    exponents = jnp.arange(half_width, dtype=jnp.float32) * (2.0 / vectors.shape[-1])
    frequency = 1.0 / jnp.power(jnp.float32(rope_base), exponents)
    angles = positions.astype(jnp.float32)[:, None] * frequency[None, :]
    cosine = jnp.cos(angles)
    sine_table = jnp.sin(angles)
    lower_half = vectors[..., :half_width]
    upper_half = vectors[..., half_width:]
    return jnp.concatenate([lower_half * cosine - upper_half * sine_table, upper_half * cosine + lower_half * sine_table], axis=-1)

def reference(cand_queries, candidate_keys, candidate_values, prefix_rotated_keys, prefix_value_matrix, lengths):
    group_width = QUERY_HEADS // KEY_VALUE_HEADS
    score_scale = 1.0 / math.sqrt(HEAD_WIDTH)
    positions = PREFIX_TOKENS + jnp.arange(CANDIDATE_SLOTS, dtype=jnp.int32)
    token_index = jnp.arange(CANDIDATE_SLOTS, dtype=jnp.int32)
    allowed = jnp.concatenate([jnp.ones((CANDIDATE_SLOTS, PREFIX_TOKENS), dtype=bool), token_index[None, :] <= token_index[:, None]], axis=1)
    prefix_heads_keys = prefix_rotated_keys.reshape(PREFIX_TOKENS, KEY_VALUE_HEADS, HEAD_WIDTH).transpose(1, 0, 2)
    prefix_heads_values = prefix_value_matrix.reshape(PREFIX_TOKENS, KEY_VALUE_HEADS, HEAD_WIDTH).transpose(1, 0, 2)
    queries_all = cand_queries.reshape(CANDIDATE_TOTAL, QUERY_HEADS, CANDIDATE_SLOTS, HEAD_WIDTH)
    joined_keys = candidate_keys.reshape(CANDIDATE_TOTAL, KEY_VALUE_HEADS, CANDIDATE_SLOTS, HEAD_WIDTH)
    joined_values = candidate_values.reshape(CANDIDATE_TOTAL, KEY_VALUE_HEADS, CANDIDATE_SLOTS, HEAD_WIDTH)

    def one_candidate(candidate_parts):
        query_rows, new_keys, new_values, length = candidate_parts
        query_rows = rotate(query_rows.astype(jnp.float32), positions).astype(jnp.bfloat16)
        new_keys = rotate(new_keys.astype(jnp.float32), positions).astype(jnp.bfloat16)
        all_keys = jnp.concatenate([prefix_heads_keys, new_keys], axis=1)
        all_values = jnp.concatenate([prefix_heads_values, new_values], axis=1)
        grouped_rows = query_rows.reshape(KEY_VALUE_HEADS, group_width, CANDIDATE_SLOTS, HEAD_WIDTH)

        def one_head(head_parts):
            head_query, head_keys, head_values = head_parts
            scores = jnp.einsum('gtd,nd->gtn', head_query.astype(jnp.float32), head_keys.astype(jnp.float32)) * score_scale
            scores = jnp.where(allowed[None], scores, -jnp.inf)
            maxima = lax.optimization_barrier(jnp.max(scores, axis=-1, keepdims=True))
            exponent = jnp.exp(scores - maxima)
            totals = lax.optimization_barrier(jnp.sum(exponent, axis=-1, keepdims=True))
            weights = exponent.astype(jnp.bfloat16)
            weighted = jnp.einsum('gtn,nd->gtd', weights.astype(jnp.float32), head_values.astype(jnp.float32))
            return weighted / totals
        head_outputs = lax.map(one_head, (grouped_rows, all_keys, all_values))
        result = head_outputs.reshape(QUERY_HEADS, CANDIDATE_SLOTS, HEAD_WIDTH)
        visible = token_index < length
        return jnp.where(visible[None, :, None], result, jnp.float32(0.0)).astype(jnp.bfloat16)
    outputs = lax.map(one_candidate, (queries_all, joined_keys, joined_values, lengths))
    return outputs.reshape(CANDIDATE_TOTAL * QUERY_HEADS, CANDIDATE_SLOTS, HEAD_WIDTH)
```

```python
import functools
import math

import jax
import jax.numpy as jnp
import numpy as np
from jax import lax
from jax.experimental import pallas as pl
from jax.experimental.pallas import tpu as pltpu
from jax.sharding import PartitionSpec as P

QUERY_HEADS = 64
KEY_VALUE_HEADS = 8
HEAD_WIDTH = 128
SLOTS = 128
PREFIX = 2048
ROPE_BASE = 500000.0
GROUP = QUERY_HEADS // KEY_VALUE_HEADS
ROWS = GROUP * SLOTS
SCALE2 = math.log2(math.e) / math.sqrt(HEAD_WIDTH)

NX, NY, NZ, ZL = 4, 4, 16, 8
MESH = pl.DeviceIdType.MESH
BLOCK = 256


def rotation_table():
    half = HEAD_WIDTH // 2
    exponents = np.arange(half, dtype=np.float32) * np.float32(2.0 / HEAD_WIDTH)
    frequency = (np.float32(1.0) / np.power(np.float32(ROPE_BASE), exponents)).astype(np.float32)
    positions = np.float32(PREFIX) + np.arange(SLOTS, dtype=np.float32)
    angles = (positions[:, None] * frequency[None, :]).astype(np.float32).astype(np.float64)
    return np.concatenate([np.cos(angles), np.sin(angles)], axis=1).astype(np.float32)


def device(x, y, z, core):
    return ((z // ZL) * 2 + core, (x * NY + y) * ZL + z % ZL)


def kernel(
    kp_hbm, vp_hbm, q_hbm, ck_hbm, cv_hbm, table_hbm, len_ref, out_ref,
    kp, vp, q, ck, cv, table, send, landed, kv0, kv1, acc, top,
    in_sem, a_send, a_recv, s1_send, s1_recv, s2_send, s2_recv, d_send, d_recv,
):
    grp, seq = lax.axis_index("grp"), lax.axis_index("seq")
    core, zh = grp % 2, grp // 2
    z = zh * ZL + seq % ZL
    y = (seq // ZL) % NY
    x = seq // (ZL * NY)

    loads = [
        pltpu.make_async_copy(s, d, in_sem.at[i])
        for i, (s, d) in enumerate(
            [(kp_hbm, kp), (vp_hbm, vp), (q_hbm, q), (ck_hbm, ck), (cv_hbm, cv), (table_hbm, table)]
        )
    ]
    for load in loads:
        load.start()

    barrier = pltpu.get_barrier_semaphore()
    far = [8, 7, 9, 6, 10, 5, 11, 4, 12, 3, 13, 2, 14, 1, 15]
    near = [1, 3, 2]
    for d in far:
        pl.semaphore_signal(barrier, inc=1, device_id=device(x, y, (z + d) % NZ, core), device_id_type=MESH)
    for d in near:
        pl.semaphore_signal(barrier, inc=1, device_id=device((x + d) % NX, y, z, core), device_id_type=MESH)
        pl.semaphore_signal(barrier, inc=1, device_id=device(x, (y + d) % NY, z, core), device_id_type=MESH)
    pl.semaphore_signal(barrier, inc=1, device_id=device(x, y, z, 1 - core), device_id_type=MESH)

    loads[0].wait()
    loads[1].wait()
    both = jnp.concatenate([kp[...].astype(jnp.float32), vp[...].astype(jnp.float32)], axis=0)
    both = both.astype(jnp.bfloat16)
    for h in range(KEY_VALUE_HEADS):
        send[h] = both[:, h * HEAD_WIDTH : (h + 1) * HEAD_WIDTH]

    pl.semaphore_wait(barrier, len(far) + 2 * len(near) + 1)

    for d in far:
        zt = (z + d) % NZ
        pltpu.make_async_remote_copy(
            src_ref=send.at[zt % ZL], dst_ref=landed.at[z], send_sem=a_send, recv_sem=a_recv,
            device_id=device(x, y, zt, core), device_id_type=MESH,
        ).start()
    pltpu.make_async_copy(send.at[z % ZL], landed.at[z], a_recv).start()

    for load in loads[2:]:
        load.wait()
    lower = lax.broadcasted_iota(jnp.int32, (SLOTS, HEAD_WIDTH), 1) < HEAD_WIDTH // 2
    cs = table[...]
    turned = pltpu.roll(cs, HEAD_WIDTH // 2, 1)
    cosine = jnp.where(lower, cs, turned)
    sine = jnp.where(lower, -turned, cs)

    def rotate(rows):
        rows = rows.astype(jnp.float32)
        return (rows * cosine + pltpu.roll(rows, HEAD_WIDTH // 2, 1) * sine).astype(jnp.bfloat16)

    new_keys = rotate(ck[...].reshape(SLOTS, HEAD_WIDTH))
    new_values = cv[...].reshape(SLOTS, HEAD_WIDTH)
    ones = jnp.ones((SLOTS, HEAD_WIDTH), jnp.bfloat16)
    new_values = jnp.concatenate([new_values, ones], axis=1)
    causal = lax.broadcasted_iota(jnp.int32, (SLOTS, SLOTS), 1) <= lax.broadcasted_iota(
        jnp.int32, (SLOTS, SLOTS), 0
    )

    def own(h, carry):
        rows = rotate(q[h])
        q[h] = rows
        s = lax.dot_general(rows, new_keys, (((1,), (1,)), ((), ())), preferred_element_type=jnp.float32)
        s = jnp.where(causal, s * SCALE2, -jnp.inf)
        m = jnp.max(s, axis=1, keepdims=True)
        p = jnp.exp2(s - m).astype(jnp.bfloat16)
        r = pl.ds(pl.multiple_of(h * SLOTS, SLOTS), SLOTS)
        acc[r, :] = jnp.dot(p, new_values, preferred_element_type=jnp.float32)
        top[r, :] = jnp.broadcast_to(m, (SLOTS, HEAD_WIDTH))
        return carry

    lax.fori_loop(0, GROUP, own, 0)

    pltpu.make_async_copy(landed, landed, a_recv).wait()
    first = lax.broadcasted_iota(jnp.int32, (8, HEAD_WIDTH), 0) < 4
    for half, ref, a, b in ((0, kv0, y, x), (1, kv1, x, y)):
        keys, values = [], []
        for i in range(half * NZ // 2, (half + 1) * NZ // 2, 2):
            even, odd = landed[i].astype(jnp.float32), landed[i + 1].astype(jnp.float32)
            keys.append(jnp.where(first, even, pltpu.roll(odd, 4, 0)))
            values.append(jnp.where(first, pltpu.roll(even, 4, 0), odd))
        ref[core, a, b, 0] = jnp.concatenate(keys, axis=0).astype(jnp.bfloat16)
        ref[core, a, b, 1] = jnp.concatenate(values, axis=0).astype(jnp.bfloat16)

    for d in near:
        pltpu.make_async_remote_copy(
            src_ref=kv0.at[core, y, x], dst_ref=kv0.at[core, y, x], send_sem=s1_send.at[0],
            recv_sem=s1_recv.at[0], device_id=device((x + d) % NX, y, z, core), device_id_type=MESH,
        ).start()
        pltpu.make_async_remote_copy(
            src_ref=kv1.at[core, x, y], dst_ref=kv1.at[core, x, y], send_sem=s1_send.at[1],
            recv_sem=s1_recv.at[1], device_id=device(x, (y + d) % NY, z, core), device_id_type=MESH,
        ).start()
    three = kv0.at[0, 0, pl.ds(0, 3)]
    pltpu.make_async_copy(three, three, s1_recv.at[0]).wait()
    pltpu.make_async_copy(three, three, s1_recv.at[1]).wait()
    for d in near:
        pltpu.make_async_remote_copy(
            src_ref=kv0.at[core, y], dst_ref=kv0.at[core, y], send_sem=s2_send.at[0],
            recv_sem=s2_recv.at[0, d - 1], device_id=device(x, (y + d) % NY, z, core), device_id_type=MESH,
        ).start()
        pltpu.make_async_remote_copy(
            src_ref=kv1.at[core, x], dst_ref=kv1.at[core, x], send_sem=s2_send.at[1],
            recv_sem=s2_recv.at[1, d - 1], device_id=device((x + d) % NX, y, z, core), device_id_type=MESH,
        ).start()

    def across(slot, yy, xx):
        for i, ref, line in ((0, kv0, yy), (1, kv1, xx)):
            pltpu.make_async_remote_copy(
                src_ref=ref.at[core, line], dst_ref=ref.at[core, line], send_sem=d_send.at[i],
                recv_sem=d_recv.at[i, slot], device_id=device(x, y, z, 1 - core), device_id_type=MESH,
            ).start()

    line = kv0.at[0, 0]

    def line_wait(sems, slot):
        for i in (0, 1):
            pltpu.make_async_copy(line, line, sems.at[i, slot]).wait()

    ones_block = jnp.ones((SLOTS, HEAD_WIDTH), jnp.bfloat16)

    def attend(parts, last=False):
        def rows_of(ref, c, l, which):
            return ref[c, l, :, which].reshape(SLOTS, HEAD_WIDTH)

        def body(i, carry):
            r = pl.ds(pl.multiple_of(i * BLOCK, BLOCK), BLOCK)
            heads = BLOCK // SLOTS
            rows = q[pl.ds(i * heads, heads)].reshape(BLOCK, HEAD_WIDTH)
            keys = jnp.concatenate([rows_of(ref, c, l, 0) for ref, c, l in parts], axis=0)
            values = jnp.concatenate(
                [jnp.concatenate([rows_of(ref, c, l, 1), ones_block], axis=1) for ref, c, l in parts], axis=0
            )
            s = lax.dot_general(rows, keys, (((1,), (1,)), ((), ())), preferred_element_type=jnp.float32)
            s = s * SCALE2
            old = top[r, :]
            m = jnp.maximum(old, jnp.max(s, axis=1, keepdims=True))
            decline = jnp.exp2(old - m)
            p = jnp.exp2(s - m[:, :1]).astype(jnp.bfloat16)
            o = acc[r, :] * jnp.concatenate([decline, decline], axis=1) + jnp.dot(
                p, values, preferred_element_type=jnp.float32
            )
            if not last:
                acc[r, :] = o
                top[r, :] = m
            else:
                mine = (grp * lax.axis_size("seq") + seq) // KEY_VALUE_HEADS
                token = lax.broadcasted_iota(jnp.int32, (BLOCK, HEAD_WIDTH), 0) % SLOTS
                result = jnp.where(token < len_ref[mine], o[:, :HEAD_WIDTH] / o[:, HEAD_WIDTH:], 0.0)
                out_ref[pl.ds(i * heads, heads)] = result.astype(jnp.bfloat16).reshape(heads, SLOTS, HEAD_WIDTH)
            return carry

        lax.fori_loop(0, ROWS // BLOCK, body, 0)

    def lines(c, yy, xx):
        return [(kv0, c, yy), (kv1, c, xx)]

    across(0, y, x)
    attend(lines(core, y, x))
    before = (0, y, x)
    for d in near:
        yy, xx = (y + NY - d) % NY, (x + NX - d) % NX
        line_wait(s2_recv, d - 1)
        across(d, yy, xx)
        line_wait(d_recv, before[0])
        attend(lines(1 - core, before[1], before[2]) + lines(core, yy, xx))
        before = (d, yy, xx)
    line_wait(d_recv, before[0])
    attend(lines(1 - core, before[1], before[2]), last=True)

    pltpu.make_async_copy(landed.at[pl.ds(0, NZ - 1)], landed.at[pl.ds(0, NZ - 1)], a_send).wait()
    lines3 = kv0.at[0, pl.ds(0, 3)]
    for i in (0, 1):
        pltpu.make_async_copy(three, three, s1_send.at[i]).wait()
        pltpu.make_async_copy(lines3, lines3, s2_send.at[i]).wait()
        pltpu.make_async_copy(kv0.at[0], kv0.at[0], d_send.at[i]).wait()


def shards(cand_queries, candidate_keys, candidate_values, prefix_keys, prefix_values, lengths):
    bf16, f32 = jnp.bfloat16, jnp.float32
    anywhere = pl.BlockSpec(memory_space=pl.ANY)
    dma = pltpu.SemaphoreType.DMA
    return pl.pallas_call(
        kernel,
        out_shape=jax.ShapeDtypeStruct(cand_queries.shape, bf16),
        in_specs=[anywhere] * 6 + [pl.BlockSpec(memory_space=pltpu.SMEM)],
        out_specs=pl.BlockSpec(memory_space=pltpu.VMEM),
        scratch_shapes=[
            pltpu.VMEM(prefix_keys.shape, bf16),
            pltpu.VMEM(prefix_values.shape, bf16),
            pltpu.VMEM(cand_queries.shape, bf16),
            pltpu.VMEM(candidate_keys.shape, bf16),
            pltpu.VMEM(candidate_values.shape, bf16),
            pltpu.VMEM((SLOTS, HEAD_WIDTH), f32),
            pltpu.VMEM((KEY_VALUE_HEADS, 8, HEAD_WIDTH), bf16),
            pltpu.VMEM((NZ, 8, HEAD_WIDTH), bf16),
            pltpu.VMEM((2, NY, NX, 2, 32, HEAD_WIDTH), bf16),
            pltpu.VMEM((2, NX, NY, 2, 32, HEAD_WIDTH), bf16),
            pltpu.VMEM((ROWS, 2 * HEAD_WIDTH), f32),
            pltpu.VMEM((ROWS, HEAD_WIDTH), f32),
            dma((6,)),
            dma,
            dma,
            dma((2,)),
            dma((2,)),
            dma((2,)),
            dma((2, 3)),
            dma((2,)),
            dma((2, 4)),
        ],
        compiler_params=pltpu.CompilerParams(
            collective_id=0, has_side_effects=True, vmem_limit_bytes=40 * 1024 * 1024
        ),
    )(prefix_keys, prefix_values, cand_queries, candidate_keys, candidate_values, jnp.asarray(rotation_table()), lengths)


def solution(mesh):
    split = P(("grp", "seq"), None, None)
    rows = P(("grp", "seq"), None)
    return jax.shard_map(
        shards,
        mesh=mesh,
        in_specs=(split, split, split, rows, rows, P()),
        out_specs=split,
        check_vma=False,
    )
```

```python
import functools
import math

import jax
import jax.numpy as jnp
import numpy as np
from jax import lax
from jax.experimental import pallas as pl
from jax.experimental.pallas import tpu as pltpu
from jax.sharding import PartitionSpec as P

QUERY_HEADS = 64
KEY_VALUE_HEADS = 8
HEAD_WIDTH = 128
SLOTS = 128
PREFIX = 2048
ROPE_BASE = 500000.0
GROUP = QUERY_HEADS // KEY_VALUE_HEADS
ROWS = GROUP * SLOTS
SCALE2 = math.log2(math.e) / math.sqrt(HEAD_WIDTH)

NX, NY, NZ, ZL = 4, 4, 16, 8
MESH = pl.DeviceIdType.MESH
BLOCK = 256
WAVES = 2
EARLY, LATE = 4, 8
PER = NZ // WAVES
OFFSETS = sorted(
    [(dx, dy) for dx in range(NX) for dy in range(NY)],
    key=lambda o: min(o[0], NX - o[0]) + min(o[1], NY - o[1]),
)
SET = 8
SETS = NX * NY // SET


def rotation_table():
    half = HEAD_WIDTH // 2
    exponents = np.arange(half, dtype=np.float32) * np.float32(2.0 / HEAD_WIDTH)
    frequency = (np.float32(1.0) / np.power(np.float32(ROPE_BASE), exponents)).astype(np.float32)
    positions = np.float32(PREFIX) + np.arange(SLOTS, dtype=np.float32)
    angles = (positions[:, None] * frequency[None, :]).astype(np.float32).astype(np.float64)
    return np.concatenate([np.cos(angles), np.sin(angles)], axis=1).astype(np.float32)


def device(x, y, z, core):
    return ((z // ZL) * 2 + core, (x * NY + y) * ZL + z % ZL)


def kernel(
    kp_hbm, vp_hbm, q_hbm, ck_hbm, cv_hbm, table_hbm, len_ref, out_ref,
    kp, vp, q, ck, cv, table, send, landed, kv, acc, top,
    in_sem, a_send, a_recv, p_send, p_recv, d_send, d_recv, ready, late_in, all_in,
):
    grp, seq = lax.axis_index("grp"), lax.axis_index("seq")
    core, zh = grp % 2, grp // 2
    z = zh * ZL + seq % ZL
    y = (seq // ZL) % NY
    x = seq // (ZL * NY)

    loads = [
        pltpu.make_async_copy(s, d, in_sem.at[i])
        for i, (s, d) in enumerate(
            [(kp_hbm, kp), (vp_hbm, vp), (q_hbm, q), (ck_hbm, ck), (cv_hbm, cv), (table_hbm, table)]
        )
    ]
    for load in loads:
        load.start()

    barrier = pltpu.get_barrier_semaphore()
    early, late = z < EARLY, z >= LATE

    def signal(sem, *place):
        pl.semaphore_signal(sem, inc=1, device_id=device(*place), device_id_type=MESH)

    for zt in range(NZ):

        @pl.when(early & (z != zt))
        def _():
            signal(barrier, x, y, zt, 1)

    @pl.when(core == 0)
    def _():
        signal(barrier, x, y, z, 1)

    loads[0].wait()
    loads[1].wait()
    both = jnp.concatenate([kp[...].astype(jnp.float32), vp[...].astype(jnp.float32)], axis=0)
    both = both.astype(jnp.bfloat16)
    for h in range(KEY_VALUE_HEADS):
        send[h] = both[:, h * HEAD_WIDTH : (h + 1) * HEAD_WIDTH]

    @pl.when(core == 1)
    def _():
        pl.semaphore_wait(barrier, jnp.where(early, 2 * EARLY - 1, 2 * EARLY + 1))
        signal(ready, x, y, z, 0)

    @pl.when(core == 0)
    def _():
        pl.semaphore_wait(ready, 1)

    def give(zt):
        pltpu.make_async_remote_copy(
            src_ref=send.at[zt % ZL], dst_ref=landed.at[z], send_sem=a_send, recv_sem=a_recv.at[z // PER],
            device_id=device(x, y, zt, core), device_id_type=MESH,
        ).start()

    for zt in range(EARLY):

        @pl.when(z != zt)
        def _():
            give(zt)

        @pl.when(late)
        def _():
            signal(late_in, x, y, zt, core)

    @pl.when(core == 0)
    def _():
        for dx, dy in OFFSETS[:0:-1]:
            signal(barrier, (x + dx) % NX, (y + dy) % NY, z, 0)
        for zt in range(NZ):
            far_end = z != zt
            if zt < EARLY:
                far_end &= ~late

            @pl.when(far_end & ~early)
            def _():
                signal(barrier, x, y, zt, 0)

    for load in loads[2:]:
        load.wait()
    lower = lax.broadcasted_iota(jnp.int32, (SLOTS, HEAD_WIDTH), 1) < HEAD_WIDTH // 2
    cs = table[...]
    turned = pltpu.roll(cs, HEAD_WIDTH // 2, 1)
    cosine = jnp.where(lower, cs, turned)
    sine = jnp.where(lower, -turned, cs)

    def rotate(rows):
        rows = rows.astype(jnp.float32)
        return (rows * cosine + pltpu.roll(rows, HEAD_WIDTH // 2, 1) * sine).astype(jnp.bfloat16)

    new_keys = rotate(ck[...].reshape(SLOTS, HEAD_WIDTH))
    new_values = cv[...].reshape(SLOTS, HEAD_WIDTH)
    ones = jnp.ones((SLOTS, HEAD_WIDTH), jnp.bfloat16)
    new_values = jnp.concatenate([new_values, ones], axis=1)
    causal = lax.broadcasted_iota(jnp.int32, (SLOTS, SLOTS), 1) <= lax.broadcasted_iota(
        jnp.int32, (SLOTS, SLOTS), 0
    )

    def own(h, carry):
        rows = rotate(q[h])
        q[h] = rows
        s = lax.dot_general(rows, new_keys, (((1,), (1,)), ((), ())), preferred_element_type=jnp.float32)
        s = jnp.where(causal, s * SCALE2, -jnp.inf)
        m = jnp.max(s, axis=1, keepdims=True)
        p = jnp.exp2(s - m).astype(jnp.bfloat16)
        r = pl.ds(pl.multiple_of(h * SLOTS, SLOTS), SLOTS)
        acc[r, :] = jnp.dot(p, new_values, preferred_element_type=jnp.float32)
        top[r, :] = jnp.broadcast_to(m, (SLOTS, HEAD_WIDTH))
        return carry

    lax.fori_loop(0, GROUP, own, 0)

    @pl.when(core == 0)
    def _():
        plane, middle = NX * NY - 1, LATE - EARLY
        others = jnp.where(early, middle, NZ - EARLY - 1)
        pl.semaphore_wait(barrier, plane + others)
        signal(all_in, x, y, z, 1)

    @pl.when(core == 1)
    def _():
        pl.semaphore_wait(all_in, 1)

    for zt in range(EARLY, NZ):
        there = z != zt
        if zt >= LATE:
            there &= ~early

        @pl.when(there)
        def _():
            give(zt)

    pltpu.make_async_copy(send.at[z % ZL], landed.at[z], a_recv.at[z // PER]).start()

    half_line = lax.broadcasted_iota(jnp.int32, (8, HEAD_WIDTH), 0) < 4
    for w in range(WAVES):
        src = (z // PER + w) % WAVES
        arrived = landed.at[pl.ds(src * PER, PER)]
        pltpu.make_async_copy(arrived, arrived, a_recv.at[src]).wait()
        keys, values = [], []
        for i in range(0, PER, 2):
            even = landed[src * PER + i].astype(jnp.float32)
            odd = landed[src * PER + i + 1].astype(jnp.float32)
            keys.append(jnp.where(half_line, even, pltpu.roll(odd, 4, 0)))
            values.append(jnp.where(half_line, pltpu.roll(even, 4, 0), odd))
        kv[w, core, 0, 0] = jnp.concatenate(keys, axis=0).astype(jnp.bfloat16)
        kv[w, core, 0, 1] = jnp.concatenate(values, axis=0).astype(jnp.bfloat16)
        for i, (dx, dy) in enumerate(OFFSETS):
            if i:
                pltpu.make_async_remote_copy(
                    src_ref=kv.at[w, core, 0], dst_ref=kv.at[w, core, i], send_sem=p_send.at[w],
                    recv_sem=p_recv.at[w, i // SET], device_id=device((x + dx) % NX, (y + dy) % NY, z, core),
                    device_id_type=MESH,
                ).start()

        if w == 0:

            @pl.when(early)
            def _():
                pl.semaphore_wait(late_in, NZ - LATE)
                for zt in range(LATE, NZ):
                    give(zt)

    ones_block = jnp.ones((SET * PER * 4, HEAD_WIDTH), jnp.bfloat16)
    mine = (grp * lax.axis_size("seq") + seq) // KEY_VALUE_HEADS

    def attend(parts, last=False):
        def rows_of(w, c, g, which):
            return kv[w, c, g * SET : (g + 1) * SET, which].reshape(SET * PER * 4, HEAD_WIDTH)

        def body(i, carry):
            r = pl.ds(pl.multiple_of(i * BLOCK, BLOCK), BLOCK)
            heads = BLOCK // SLOTS
            rows = q[pl.ds(i * heads, heads)].reshape(BLOCK, HEAD_WIDTH)
            keys = jnp.concatenate([rows_of(*p, 0) for p in parts], axis=0)
            values = jnp.concatenate(
                [jnp.concatenate([rows_of(*p, 1), ones_block], axis=1) for p in parts], axis=0
            )
            s = lax.dot_general(rows, keys, (((1,), (1,)), ((), ())), preferred_element_type=jnp.float32)
            s = s * SCALE2
            old = top[r, :]
            m = jnp.maximum(old, jnp.max(s, axis=1, keepdims=True))
            decline = jnp.exp2(old - m)
            p = jnp.exp2(s - m[:, :1]).astype(jnp.bfloat16)
            o = acc[r, :] * jnp.concatenate([decline, decline], axis=1) + jnp.dot(
                p, values, preferred_element_type=jnp.float32
            )
            if not last:
                acc[r, :] = o
                top[r, :] = m
            else:
                token = lax.broadcasted_iota(jnp.int32, (BLOCK, HEAD_WIDTH), 0) % SLOTS
                result = jnp.where(token < len_ref[mine], o[:, :HEAD_WIDTH] / o[:, HEAD_WIDTH:], 0.0)
                out_ref[pl.ds(i * heads, heads)] = result.astype(jnp.bfloat16).reshape(heads, SLOTS, HEAD_WIDTH)
            return carry

        lax.fori_loop(0, ROWS // BLOCK, body, 0)

    before = None
    for w in range(WAVES):
        for g in range(SETS):
            whole = kv.at[w, core, pl.ds(g * SET, SET)]
            if g:
                pltpu.make_async_copy(whole, whole, p_recv.at[w, g]).wait()
            else:
                rest = kv.at[w, core, pl.ds(1, SET - 1)]
                pltpu.make_async_copy(rest, rest, p_recv.at[w, g]).wait()
            pltpu.make_async_remote_copy(
                src_ref=whole, dst_ref=whole, send_sem=d_send, recv_sem=d_recv.at[w, g],
                device_id=device(x, y, z, 1 - core), device_id_type=MESH,
            ).start()
            if before is not None:
                pltpu.make_async_copy(whole, whole, d_recv.at[before[0], before[1]]).wait()
                attend([(before[0], 1 - core, before[1]), (w, core, g)])
            else:
                attend([(w, core, g)])
            before = (w, g)
    pltpu.make_async_copy(whole, whole, d_recv.at[before[0], before[1]]).wait()
    attend([(before[0], 1 - core, before[1])], last=True)

    pltpu.make_async_copy(landed.at[pl.ds(0, NZ - 1)], landed.at[pl.ds(0, NZ - 1)], a_send).wait()
    for w in range(WAVES):
        sent = kv.at[w, 0, pl.ds(1, NX * NY - 1)]
        pltpu.make_async_copy(sent, sent, p_send.at[w]).wait()
    pltpu.make_async_copy(kv.at[:, 0], kv.at[:, 0], d_send).wait()


def shards(cand_queries, candidate_keys, candidate_values, prefix_keys, prefix_values, lengths):
    bf16, f32 = jnp.bfloat16, jnp.float32
    anywhere = pl.BlockSpec(memory_space=pl.ANY)
    dma = pltpu.SemaphoreType.DMA
    return pl.pallas_call(
        kernel,
        out_shape=pltpu.VMEM(cand_queries.shape, bf16),
        in_specs=[anywhere] * 6 + [pl.BlockSpec(memory_space=pltpu.SMEM)],
        out_specs=pl.BlockSpec(memory_space=pltpu.VMEM),
        scratch_shapes=[
            pltpu.VMEM(prefix_keys.shape, bf16),
            pltpu.VMEM(prefix_values.shape, bf16),
            pltpu.VMEM(cand_queries.shape, bf16),
            pltpu.VMEM(candidate_keys.shape, bf16),
            pltpu.VMEM(candidate_values.shape, bf16),
            pltpu.VMEM((SLOTS, HEAD_WIDTH), f32),
            pltpu.VMEM((KEY_VALUE_HEADS, 8, HEAD_WIDTH), bf16),
            pltpu.VMEM((NZ, 8, HEAD_WIDTH), bf16),
            pltpu.VMEM((WAVES, 2, NX * NY, 2, PER * 4, HEAD_WIDTH), bf16),
            pltpu.VMEM((ROWS, 2 * HEAD_WIDTH), f32),
            pltpu.VMEM((ROWS, HEAD_WIDTH), f32),
            dma((6,)),
            dma,
            dma((WAVES,)),
            dma((WAVES,)),
            dma((WAVES, SETS)),
            dma,
            dma((WAVES, SETS)),
            pltpu.SemaphoreType.REGULAR,
            pltpu.SemaphoreType.REGULAR,
            pltpu.SemaphoreType.REGULAR,
        ],
        compiler_params=pltpu.CompilerParams(
            collective_id=0, has_side_effects=True, vmem_limit_bytes=60 * 1024 * 1024
        ),
    )(prefix_keys, prefix_values, cand_queries, candidate_keys, candidate_values, jnp.asarray(rotation_table()), lengths)


def solution(mesh):
    split = P(("grp", "seq"), None, None)
    rows = P(("grp", "seq"), None)
    return jax.shard_map(
        shards,
        mesh=mesh,
        in_specs=(split, split, split, rows, rows, P()),
        out_specs=split,
        check_vma=False,
    )
```

```python
import functools
import math

import jax
import jax.numpy as jnp
import numpy as np
from jax import lax
from jax.experimental import pallas as pl
from jax.experimental.pallas import tpu as pltpu
from jax.sharding import PartitionSpec as P

QUERY_HEADS = 64
KEY_VALUE_HEADS = 8
HEAD_WIDTH = 128
SLOTS = 128
PREFIX = 2048
ROPE_BASE = 500000.0
GROUP = QUERY_HEADS // KEY_VALUE_HEADS
ROWS = GROUP * SLOTS
SCALE2 = math.log2(math.e) / math.sqrt(HEAD_WIDTH)

NX, NY, NZ, ZL = 4, 4, 16, 8
MESH = pl.DeviceIdType.MESH
WAVES = 2
EARLY, LATE = 5, 8
PER = NZ // WAVES
OFFSETS = sorted(
    [(dx, dy) for dx in range(NX) for dy in range(NY)],
    key=lambda o: -(min(o[0], NX - o[0]) + min(o[1], NY - o[1])) if any(o) else -99,
)
SET = 8
SETS = NX * NY // SET


def rotation_table():
    half = HEAD_WIDTH // 2
    exponents = np.arange(half, dtype=np.float32) * np.float32(2.0 / HEAD_WIDTH)
    frequency = (np.float32(1.0) / np.power(np.float32(ROPE_BASE), exponents)).astype(np.float32)
    positions = np.float32(PREFIX) + np.arange(SLOTS, dtype=np.float32)
    angles = (positions[:, None] * frequency[None, :]).astype(np.float32).astype(np.float64)
    return np.concatenate([np.cos(angles), np.sin(angles)], axis=1).astype(np.float32)


def device(x, y, z, core):
    return ((z // ZL) * 2 + core, (x * NY + y) * ZL + z % ZL)


def kernel(
    kp_hbm, vp_hbm, q_hbm, ck_hbm, cv_hbm, table_hbm, len_ref, out_ref,
    kp, vp, q, ck, cv, table, send, landed, kv, acc, top,
    in_sem, a_send, a_recv, p_send, p_recv, d_send, d_recv, ready, late_in, all_in,
):
    grp, seq = lax.axis_index("grp"), lax.axis_index("seq")
    core, zh = grp % 2, grp // 2
    z = zh * ZL + seq % ZL
    y = (seq // ZL) % NY
    x = seq // (ZL * NY)

    loads = [
        pltpu.make_async_copy(s, d, in_sem.at[i])
        for i, (s, d) in enumerate(
            [(kp_hbm, kp), (vp_hbm, vp), (q_hbm, q), (ck_hbm, ck), (cv_hbm, cv), (table_hbm, table)]
        )
    ]
    for load in loads:
        load.start()

    barrier = pltpu.get_barrier_semaphore()
    early, late = z < EARLY, z >= LATE

    def signal(sem, *place):
        pl.semaphore_signal(sem, inc=1, device_id=device(*place), device_id_type=MESH)

    for zt in range(NZ):

        @pl.when(early & (z != zt))
        def _():
            signal(barrier, x, y, zt, 1)

    @pl.when(core == 0)
    def _():
        signal(barrier, x, y, z, 1)

    loads[0].wait()
    loads[1].wait()
    both = jnp.concatenate([kp[...].astype(jnp.float32), vp[...].astype(jnp.float32)], axis=0)
    both = both.astype(jnp.bfloat16)
    for h in range(KEY_VALUE_HEADS):
        send[h] = both[:, h * HEAD_WIDTH : (h + 1) * HEAD_WIDTH]

    @pl.when(core == 1)
    def _():
        pl.semaphore_wait(barrier, jnp.where(early, 2 * EARLY - 1, 2 * EARLY + 1))
        signal(ready, x, y, z, 0)

    @pl.when(core == 0)
    def _():
        pl.semaphore_wait(ready, 1)

    def give(zt):
        pltpu.make_async_remote_copy(
            src_ref=send.at[zt % ZL], dst_ref=landed.at[z], send_sem=a_send, recv_sem=a_recv.at[z // PER],
            device_id=device(x, y, zt, core), device_id_type=MESH,
        ).start()

    for zt in range(EARLY):

        @pl.when(z != zt)
        def _():
            give(zt)

        @pl.when(late)
        def _():
            signal(late_in, x, y, zt, core)

    @pl.when(core == 0)
    def _():
        for dx, dy in OFFSETS[1:]:
            signal(barrier, (x + dx) % NX, (y + dy) % NY, z, 0)
        for zt in range(NZ):
            far_end = z != zt
            if zt < EARLY:
                far_end &= ~late

            @pl.when(far_end & ~early)
            def _():
                signal(barrier, x, y, zt, 0)

    for load in loads[2:]:
        load.wait()
    lower = lax.broadcasted_iota(jnp.int32, (SLOTS, HEAD_WIDTH), 1) < HEAD_WIDTH // 2
    cs = table[...]
    turned = pltpu.roll(cs, HEAD_WIDTH // 2, 1)
    cosine = jnp.where(lower, cs, turned)
    sine = jnp.where(lower, -turned, cs)

    def rotate(rows):
        rows = rows.astype(jnp.float32)
        return (rows * cosine + pltpu.roll(rows, HEAD_WIDTH // 2, 1) * sine).astype(jnp.bfloat16)

    new_keys = rotate(ck[...].reshape(SLOTS, HEAD_WIDTH))
    new_values = cv[...].reshape(SLOTS, HEAD_WIDTH)
    ones = jnp.ones((SLOTS, HEAD_WIDTH), jnp.bfloat16)
    new_values = jnp.concatenate([new_values, ones], axis=1)
    causal = lax.broadcasted_iota(jnp.int32, (SLOTS, SLOTS), 1) <= lax.broadcasted_iota(
        jnp.int32, (SLOTS, SLOTS), 0
    )

    def own(h):
        rows = rotate(q[h])
        q[h] = rows
        s = lax.dot_general(rows, new_keys, (((1,), (1,)), ((), ())), preferred_element_type=jnp.float32)
        s = jnp.where(causal, s * SCALE2, -jnp.inf)
        m = jnp.max(s, axis=1, keepdims=True)
        p = jnp.exp2(s - m).astype(jnp.bfloat16)
        r = pl.ds(h * SLOTS, SLOTS)
        acc[r, :] = jnp.dot(p, new_values, preferred_element_type=jnp.float32)
        top[r, :] = jnp.broadcast_to(m, (SLOTS, HEAD_WIDTH))

    for h in range(GROUP):
        own(h)

    @pl.when(core == 0)
    def _():
        plane, middle = NX * NY - 1, LATE - EARLY
        others = jnp.where(early, middle, NZ - EARLY - 1)
        pl.semaphore_wait(barrier, plane + others)
        signal(all_in, x, y, z, 1)

    @pl.when(core == 1)
    def _():
        pl.semaphore_wait(all_in, 1)

    for zt in range(EARLY, NZ):
        there = z != zt
        if zt >= LATE:
            there &= ~early

        @pl.when(there)
        def _():
            give(zt)

    pltpu.make_async_copy(send.at[z % ZL], landed.at[z], a_recv.at[z // PER]).start()

    half_line = lax.broadcasted_iota(jnp.int32, (8, HEAD_WIDTH), 0) < 4
    for w in range(WAVES):
        src = (z // PER + w) % WAVES
        arrived = landed.at[pl.ds(src * PER, PER)]
        pltpu.make_async_copy(arrived, arrived, a_recv.at[src]).wait()
        keys, values = [], []
        for i in range(0, PER, 2):
            even = landed[src * PER + i].astype(jnp.float32)
            odd = landed[src * PER + i + 1].astype(jnp.float32)
            keys.append(jnp.where(half_line, even, pltpu.roll(odd, 4, 0)))
            values.append(jnp.where(half_line, pltpu.roll(even, 4, 0), odd))
        kv[w, core, 0, 0] = jnp.concatenate(keys, axis=0).astype(jnp.bfloat16)
        kv[w, core, 0, 1] = jnp.concatenate(values, axis=0).astype(jnp.bfloat16)
        for i, (dx, dy) in enumerate(OFFSETS):
            if i:
                pltpu.make_async_remote_copy(
                    src_ref=kv.at[w, core, 0], dst_ref=kv.at[w, core, i], send_sem=p_send.at[w],
                    recv_sem=p_recv.at[w, i // SET], device_id=device((x + dx) % NX, (y + dy) % NY, z, core),
                    device_id_type=MESH,
                ).start()

        if w == 0:

            @pl.when(early)
            def _():
                pl.semaphore_wait(late_in, NZ - LATE)
                for zt in range(LATE, NZ):
                    give(zt)

    keys_here = SET * PER * 4
    ones_block = jnp.ones((keys_here, HEAD_WIDTH), jnp.bfloat16)
    mine = (grp * lax.axis_size("seq") + seq) // KEY_VALUE_HEADS

    def attend(w, c, g, last=False):
        block = kv[w, c, g * SET : (g + 1) * SET]
        keys = block[:, 0].reshape(keys_here, HEAD_WIDTH)
        values = jnp.concatenate([block[:, 1].reshape(keys_here, HEAD_WIDTH), ones_block], axis=1)
        s = lax.dot_general(
            q[...].reshape(ROWS, HEAD_WIDTH), keys, (((1,), (1,)), ((), ())), preferred_element_type=jnp.float32
        )
        tiles = [s[:, t : t + HEAD_WIDTH] for t in range(0, keys_here, HEAD_WIDTH)]
        old = top[...]
        m = jnp.maximum(old, jnp.max(functools.reduce(jnp.maximum, tiles), axis=1, keepdims=True) * SCALE2)
        decline = jnp.exp2(old - m)
        p = jnp.concatenate([jnp.exp2(t * SCALE2 - m).astype(jnp.bfloat16) for t in tiles], axis=1)
        o = acc[...] * jnp.concatenate([decline, decline], axis=1) + jnp.dot(
            p, values, preferred_element_type=jnp.float32
        )
        if not last:
            acc[...] = o
            top[...] = m
        else:
            token = lax.broadcasted_iota(jnp.int32, (ROWS, HEAD_WIDTH), 0) % SLOTS
            result = jnp.where(token < len_ref[mine], o[:, :HEAD_WIDTH] / o[:, HEAD_WIDTH:], 0.0)
            out_ref[...] = result.astype(jnp.bfloat16).reshape(GROUP, SLOTS, HEAD_WIDTH)

    before = None
    for w in range(WAVES):
        for g in range(SETS):
            whole = kv.at[w, core, pl.ds(g * SET, SET)]
            if g:
                pltpu.make_async_copy(whole, whole, p_recv.at[w, g]).wait()
            else:
                rest = kv.at[w, core, pl.ds(1, SET - 1)]
                pltpu.make_async_copy(rest, rest, p_recv.at[w, g]).wait()
            pltpu.make_async_remote_copy(
                src_ref=whole, dst_ref=whole, send_sem=d_send, recv_sem=d_recv.at[w, g],
                device_id=device(x, y, z, 1 - core), device_id_type=MESH,
            ).start()
            if before is not None:
                pltpu.make_async_copy(whole, whole, d_recv.at[before[0], before[1]]).wait()
                attend(before[0], 1 - core, before[1])
            attend(w, core, g)
            before = (w, g)
    pltpu.make_async_copy(whole, whole, d_recv.at[before[0], before[1]]).wait()
    attend(before[0], 1 - core, before[1], last=True)

    pltpu.make_async_copy(landed.at[pl.ds(0, NZ - 1)], landed.at[pl.ds(0, NZ - 1)], a_send).wait()
    for w in range(WAVES):
        sent = kv.at[w, 0, pl.ds(1, NX * NY - 1)]
        pltpu.make_async_copy(sent, sent, p_send.at[w]).wait()
    pltpu.make_async_copy(kv.at[:, 0], kv.at[:, 0], d_send).wait()


def shards(cand_queries, candidate_keys, candidate_values, prefix_keys, prefix_values, lengths):
    bf16, f32 = jnp.bfloat16, jnp.float32
    anywhere = pl.BlockSpec(memory_space=pl.ANY)
    dma = pltpu.SemaphoreType.DMA
    return pl.pallas_call(
        kernel,
        out_shape=pltpu.VMEM(cand_queries.shape, bf16),
        in_specs=[anywhere] * 6 + [pl.BlockSpec(memory_space=pltpu.SMEM)],
        out_specs=pl.BlockSpec(memory_space=pltpu.VMEM),
        scratch_shapes=[
            pltpu.VMEM(prefix_keys.shape, bf16),
            pltpu.VMEM(prefix_values.shape, bf16),
            pltpu.VMEM(cand_queries.shape, bf16),
            pltpu.VMEM(candidate_keys.shape, bf16),
            pltpu.VMEM(candidate_values.shape, bf16),
            pltpu.VMEM((SLOTS, HEAD_WIDTH), f32),
            pltpu.VMEM((KEY_VALUE_HEADS, 8, HEAD_WIDTH), bf16),
            pltpu.VMEM((NZ, 8, HEAD_WIDTH), bf16),
            pltpu.VMEM((WAVES, 2, NX * NY, 2, PER * 4, HEAD_WIDTH), bf16),
            pltpu.VMEM((ROWS, 2 * HEAD_WIDTH), f32),
            pltpu.VMEM((ROWS, HEAD_WIDTH), f32),
            dma((6,)),
            dma,
            dma((WAVES,)),
            dma((WAVES,)),
            dma((WAVES, SETS)),
            dma,
            dma((WAVES, SETS)),
            pltpu.SemaphoreType.REGULAR,
            pltpu.SemaphoreType.REGULAR,
            pltpu.SemaphoreType.REGULAR,
        ],
        compiler_params=pltpu.CompilerParams(
            collective_id=0, has_side_effects=True, vmem_limit_bytes=60 * 1024 * 1024
        ),
    )(prefix_keys, prefix_values, cand_queries, candidate_keys, candidate_values, jnp.asarray(rotation_table()), lengths)


def solution(mesh):
    split = P(("grp", "seq"), None, None)
    rows = P(("grp", "seq"), None)
    return jax.shard_map(
        shards,
        mesh=mesh,
        in_specs=(split, split, split, rows, rows, P()),
        out_specs=split,
        check_vma=False,
    )
```

```python
import functools
import math

import jax
import jax.numpy as jnp
import numpy as np
from jax import lax
from jax.experimental import pallas as pl
from jax.experimental.pallas import tpu as pltpu
from jax.sharding import PartitionSpec as P

QUERY_HEADS = 64
KEY_VALUE_HEADS = 8
HEAD_WIDTH = 128
SLOTS = 128
PREFIX = 2048
ROPE_BASE = 500000.0
GROUP = QUERY_HEADS // KEY_VALUE_HEADS
ROWS = GROUP * SLOTS
SCALE2 = math.log2(math.e) / math.sqrt(HEAD_WIDTH)

NX, NY, NZ, ZL = 4, 4, 16, 8
MESH = pl.DeviceIdType.MESH
WAVES = 4
EARLY, LATE = 4, 8
PER = NZ // WAVES
OFFSETS = sorted(
    [(dx, dy) for dx in range(NX) for dy in range(NY)],
    key=lambda o: -(min(o[0], NX - o[0]) + min(o[1], NY - o[1])) if any(o) else -99,
)


def rotation_table():
    half = HEAD_WIDTH // 2
    exponents = np.arange(half, dtype=np.float32) * np.float32(2.0 / HEAD_WIDTH)
    frequency = (np.float32(1.0) / np.power(np.float32(ROPE_BASE), exponents)).astype(np.float32)
    positions = np.float32(PREFIX) + np.arange(SLOTS, dtype=np.float32)
    angles = (positions[:, None] * frequency[None, :]).astype(np.float32).astype(np.float64)
    return np.concatenate([np.cos(angles), np.sin(angles)], axis=1).astype(np.float32)


def device(x, y, z, core):
    return ((z // ZL) * 2 + core, (x * NY + y) * ZL + z % ZL)


def kernel(
    kp_hbm, vp_hbm, q_hbm, ck_hbm, cv_hbm, table_hbm, len_ref, out_ref,
    q, ck, cv, table, landed, kv, acc, top,
    in_sem, a_send, a_recv, p_send, p_recv, d_send, d_recv, ready, late_in, all_in,
):
    grp, seq = lax.axis_index("grp"), lax.axis_index("seq")
    core, zh = grp % 2, grp // 2
    z = zh * ZL + seq % ZL
    y = (seq // ZL) % NY
    x = seq // (ZL * NY)

    loads = [
        pltpu.make_async_copy(s, d, in_sem.at[i])
        for i, (s, d) in enumerate(
            [(q_hbm, q), (ck_hbm, ck), (cv_hbm, cv), (table_hbm, table)]
        )
    ]
    for load in loads:
        load.start()

    barrier = pltpu.get_barrier_semaphore()
    early, late = z < EARLY, z >= LATE

    def signal(sem, *place):
        pl.semaphore_signal(sem, inc=1, device_id=device(*place), device_id_type=MESH)

    for zt in range(NZ):

        @pl.when(early & (z != zt))
        def _():
            signal(barrier, x, y, zt, 0)

    @pl.when(core == 1)
    def _():
        signal(barrier, x, y, z, 0)

    @pl.when(core == 0)
    def _():
        pl.semaphore_wait(barrier, jnp.where(early, 2 * EARLY - 1, 2 * EARLY + 1))
        signal(ready, x, y, z, 1)

    @pl.when(core == 1)
    def _():
        pl.semaphore_wait(ready, 1)

    def give(zt):
        head = pl.ds(zt % ZL * HEAD_WIDTH, HEAD_WIDTH)
        for i, ref in enumerate((kp_hbm, vp_hbm)):
            pltpu.make_async_remote_copy(
                src_ref=ref.at[:, head], dst_ref=landed.at[z, i], send_sem=a_send, recv_sem=a_recv.at[z // PER],
                device_id=device(x, y, zt, core), device_id_type=MESH,
            ).start()

    for zt in range(EARLY):

        @pl.when(z != zt)
        def _():
            give(zt)

    for zt in range(EARLY):

        @pl.when(late)
        def _():
            signal(late_in, x, y, zt, core)

    @pl.when(core == 1)
    def _():
        for dx, dy in OFFSETS[1:]:
            signal(barrier, (x + dx) % NX, (y + dy) % NY, z, 1)
        for zt in range(NZ):
            far_end = z != zt
            if zt < EARLY:
                far_end &= ~late

            @pl.when(far_end & ~early)
            def _():
                signal(barrier, x, y, zt, 1)

    head = pl.ds(pl.multiple_of(z % ZL * HEAD_WIDTH, HEAD_WIDTH), HEAD_WIDTH)
    for i, ref in enumerate((kp_hbm, vp_hbm)):
        pltpu.make_async_copy(ref.at[:, head], landed.at[z, i], a_recv.at[z // PER]).start()

    for load in loads:
        load.wait()
    lower = lax.broadcasted_iota(jnp.int32, (SLOTS, HEAD_WIDTH), 1) < HEAD_WIDTH // 2
    cs = table[...]
    turned = pltpu.roll(cs, HEAD_WIDTH // 2, 1)
    cosine = jnp.where(lower, cs, turned)
    sine = jnp.where(lower, -turned, cs)

    def rotate(rows):
        rows = rows.astype(jnp.float32)
        return (rows * cosine + pltpu.roll(rows, HEAD_WIDTH // 2, 1) * sine).astype(jnp.bfloat16)

    new_keys = rotate(ck[...].reshape(SLOTS, HEAD_WIDTH))
    new_values = cv[...].reshape(SLOTS, HEAD_WIDTH)
    ones = jnp.ones((SLOTS, HEAD_WIDTH), jnp.bfloat16)
    new_values = jnp.concatenate([new_values, ones], axis=1)
    causal = lax.broadcasted_iota(jnp.int32, (SLOTS, SLOTS), 1) <= lax.broadcasted_iota(
        jnp.int32, (SLOTS, SLOTS), 0
    )

    def own(h):
        rows = rotate(q[h])
        q[h] = rows
        s = lax.dot_general(rows, new_keys, (((1,), (1,)), ((), ())), preferred_element_type=jnp.float32)
        s = jnp.where(causal, s * SCALE2, -jnp.inf)
        m = jnp.max(s, axis=1, keepdims=True)
        p = jnp.exp2(s - m).astype(jnp.bfloat16)
        r = pl.ds(h * SLOTS, SLOTS)
        acc[r, :] = jnp.dot(p, new_values, preferred_element_type=jnp.float32)
        top[r, :] = jnp.broadcast_to(m, (SLOTS, HEAD_WIDTH))

    for h in range(GROUP):
        own(h)

    @pl.when(core == 1)
    def _():
        plane, middle = NX * NY - 1, LATE - EARLY
        others = jnp.where(early, middle, NZ - EARLY - 1)
        pl.semaphore_wait(barrier, plane + others)
        signal(all_in, x, y, z, 0)

    @pl.when(core == 0)
    def _():
        pl.semaphore_wait(all_in, 1)

    for zt in range(EARLY, NZ):
        there = z != zt
        if zt >= LATE:
            there &= ~early

        @pl.when(there)
        def _():
            give(zt)

    def quarter(w):
        own = z // PER
        near = jnp.where(z < 2, (0, 3, 1, 2)[w], (0, 1, 3, 2)[w])
        far = (own, 5 - own, 0, 1)[w]
        return jnp.where(early, near, jnp.where(z < NZ // 2, (0, 1, 3, 2)[w], far))

    place = x * NY + y
    for w in range(WAVES):
        src = quarter(w)
        arrived = landed.at[pl.ds(src * PER, PER)]
        pltpu.make_async_copy(arrived, arrived, a_recv.at[src]).wait()
        for which in (0, 1):
            rows = [landed[src * PER + i, which].astype(jnp.float32) for i in range(PER)]
            kv[w, core, place, which] = jnp.concatenate(rows, axis=0).astype(jnp.bfloat16)
        def pass_on(tx, ty):
            pltpu.make_async_remote_copy(
                src_ref=kv.at[w, core, place], dst_ref=kv.at[w, core, place], send_sem=p_send.at[w],
                recv_sem=p_recv.at[w], device_id=device(tx, ty, z, core), device_id_type=MESH,
            ).start()

        @pl.when(place != 0)
        def _():
            pass_on(0, 0)

        for dx, dy in OFFSETS[1:]:
            tx, ty = (x + dx) % NX, (y + dy) % NY

            @pl.when(tx + ty != 0)
            def _():
                pass_on(tx, ty)

        if w == 1:

            @pl.when(early)
            def _():
                pl.semaphore_wait(late_in, NZ - LATE)
                for zt in range(LATE, NZ):
                    give(zt)

    keys_here = NX * NY * PER * 4
    ones_block = jnp.ones((keys_here, HEAD_WIDTH), jnp.bfloat16)
    mine = (grp * lax.axis_size("seq") + seq) // KEY_VALUE_HEADS

    def attend(w, c, last=False):
        block = kv[w, c]
        keys = block[:, 0].reshape(keys_here, HEAD_WIDTH)
        values = jnp.concatenate([block[:, 1].reshape(keys_here, HEAD_WIDTH), ones_block], axis=1)
        s = lax.dot_general(
            q[...].reshape(ROWS, HEAD_WIDTH), keys, (((1,), (1,)), ((), ())), preferred_element_type=jnp.float32
        )
        tiles = [s[:, t : t + HEAD_WIDTH] for t in range(0, keys_here, HEAD_WIDTH)]
        old = top[...]
        m = jnp.maximum(old, jnp.max(functools.reduce(jnp.maximum, tiles), axis=1, keepdims=True) * SCALE2)
        decline = jnp.exp2(old - m)
        p = jnp.concatenate([jnp.exp2(t * SCALE2 - m).astype(jnp.bfloat16) for t in tiles], axis=1)
        o = acc[...] * jnp.concatenate([decline, decline], axis=1) + jnp.dot(
            p, values, preferred_element_type=jnp.float32
        )
        if not last:
            acc[...] = o
            top[...] = m
        else:
            token = lax.broadcasted_iota(jnp.int32, (ROWS, HEAD_WIDTH), 0) % SLOTS
            result = jnp.where(token < len_ref[mine], o[:, :HEAD_WIDTH] / o[:, HEAD_WIDTH:], 0.0)
            out_ref[...] = result.astype(jnp.bfloat16).reshape(GROUP, SLOTS, HEAD_WIDTH)

    peers = NX * NY - 1
    for w in range(WAVES):
        rest = kv.at[w, core, pl.ds(0, peers)]
        pltpu.make_async_copy(rest, rest, p_recv.at[w]).wait()
        whole = kv.at[w, core]
        pltpu.make_async_remote_copy(
            src_ref=whole, dst_ref=whole, send_sem=d_send, recv_sem=d_recv.at[w],
            device_id=device(x, y, z, 1 - core), device_id_type=MESH,
        ).start()
        if w:
            pltpu.make_async_copy(whole, whole, d_recv.at[w - 1]).wait()
            attend(w - 1, 1 - core)
        attend(w, core)
    pltpu.make_async_copy(whole, whole, d_recv.at[WAVES - 1]).wait()
    attend(WAVES - 1, 1 - core, last=True)

    given = landed.at[pl.ds(0, NZ - 1)]
    pltpu.make_async_copy(given, given, a_send).wait()
    for w in range(WAVES):
        sent = kv.at[w, 0, pl.ds(0, peers)]
        pltpu.make_async_copy(sent, sent, p_send.at[w]).wait()
    pltpu.make_async_copy(kv.at[:, 0], kv.at[:, 0], d_send).wait()


def shards(cand_queries, candidate_keys, candidate_values, prefix_keys, prefix_values, lengths):
    bf16, f32 = jnp.bfloat16, jnp.float32
    anywhere = pl.BlockSpec(memory_space=pl.ANY)
    dma = pltpu.SemaphoreType.DMA
    return pl.pallas_call(
        kernel,
        out_shape=pltpu.VMEM(cand_queries.shape, bf16),
        in_specs=[anywhere] * 6 + [pl.BlockSpec(memory_space=pltpu.SMEM)],
        out_specs=pl.BlockSpec(memory_space=pltpu.VMEM),
        scratch_shapes=[
            pltpu.VMEM(cand_queries.shape, bf16),
            pltpu.VMEM(candidate_keys.shape, bf16),
            pltpu.VMEM(candidate_values.shape, bf16),
            pltpu.VMEM((SLOTS, HEAD_WIDTH), f32),
            pltpu.VMEM((NZ, 2, 4, HEAD_WIDTH), bf16),
            pltpu.VMEM((WAVES, 2, NX * NY, 2, PER * 4, HEAD_WIDTH), bf16),
            pltpu.VMEM((ROWS, 2 * HEAD_WIDTH), f32),
            pltpu.VMEM((ROWS, HEAD_WIDTH), f32),
            dma((4,)),
            dma,
            dma((WAVES,)),
            dma((WAVES,)),
            dma((WAVES,)),
            dma,
            dma((WAVES,)),
            pltpu.SemaphoreType.REGULAR,
            pltpu.SemaphoreType.REGULAR,
            pltpu.SemaphoreType.REGULAR,
        ],
        compiler_params=pltpu.CompilerParams(
            collective_id=0, has_side_effects=True, vmem_limit_bytes=60 * 1024 * 1024
        ),
    )(prefix_keys, prefix_values, cand_queries, candidate_keys, candidate_values, jnp.asarray(rotation_table()), lengths)


def solution(mesh):
    split = P(("grp", "seq"), None, None)
    rows = P(("grp", "seq"), None)
    return jax.shard_map(
        shards,
        mesh=mesh,
        in_specs=(split, split, split, rows, rows, P()),
        out_specs=split,
        check_vma=False,
    )
```

```python
import functools
import math

import jax
import jax.numpy as jnp
import numpy as np
from jax import lax
from jax.experimental import pallas as pl
from jax.experimental.pallas import tpu as pltpu
from jax.sharding import PartitionSpec as P

QUERY_HEADS = 64
KEY_VALUE_HEADS = 8
HEAD_WIDTH = 128
SLOTS = 128
PREFIX = 2048
ROPE_BASE = 500000.0
GROUP = QUERY_HEADS // KEY_VALUE_HEADS
ROWS = GROUP * SLOTS
SCALE2 = math.log2(math.e) / math.sqrt(HEAD_WIDTH)

NX, NY, NZ, ZL = 4, 4, 16, 8
MESH = pl.DeviceIdType.MESH
WAVES = 4
EARLY, LATE = 4, 8
PER = NZ // WAVES
OFFSETS = sorted(
    [(dx, dy) for dx in range(NX) for dy in range(NY)],
    key=lambda o: -(min(o[0], NX - o[0]) + min(o[1], NY - o[1])) if any(o) else -99,
)


def rotation_table():
    half = HEAD_WIDTH // 2
    exponents = np.arange(half, dtype=np.float32) * np.float32(2.0 / HEAD_WIDTH)
    frequency = (np.float32(1.0) / np.power(np.float32(ROPE_BASE), exponents)).astype(np.float32)
    positions = np.float32(PREFIX) + np.arange(SLOTS, dtype=np.float32)
    angles = (positions[:, None] * frequency[None, :]).astype(np.float32).astype(np.float64)
    return np.concatenate([np.cos(angles), np.sin(angles)], axis=1).astype(np.float32)


def device(x, y, z, core):
    return ((z // ZL) * 2 + core, (x * NY + y) * ZL + z % ZL)


def kernel(
    kp_hbm, vp_hbm, q_hbm, ck_hbm, cv_hbm, table_hbm, len_ref, out_ref,
    q, ck, cv, table, landed, kv, acc, top,
    in_sem, a_send, a_recv, p_send, p_recv, d_send, d_recv, e_send, ready, late_in, all_in,
):
    grp, seq = lax.axis_index("grp"), lax.axis_index("seq")
    core, zh = grp % 2, grp // 2
    z = zh * ZL + seq % ZL
    y = (seq // ZL) % NY
    x = seq // (ZL * NY)

    loads = [
        pltpu.make_async_copy(s, d, in_sem.at[i])
        for i, (s, d) in enumerate(
            [(q_hbm, q), (ck_hbm, ck), (cv_hbm, cv), (table_hbm, table)]
        )
    ]
    for load in loads:
        load.start()

    barrier = pltpu.get_barrier_semaphore()
    early, late = z < EARLY, z >= LATE

    def signal(sem, *place):
        pl.semaphore_signal(sem, inc=1, device_id=device(*place), device_id_type=MESH)

    for zt in range(NZ):

        @pl.when(early & (z != zt))
        def _():
            signal(barrier, x, y, zt, 0)

    @pl.when(core == 1)
    def _():
        signal(barrier, x, y, z, 0)

    @pl.when(core == 0)
    def _():
        pl.semaphore_wait(barrier, jnp.where(early, 2 * EARLY - 1, 2 * EARLY + 1))
        signal(ready, x, y, z, 1)

    @pl.when(core == 1)
    def _():
        pl.semaphore_wait(ready, 1)

    def give(zt):
        head = pl.ds(zt % ZL * HEAD_WIDTH, HEAD_WIDTH)
        for i, ref in enumerate((kp_hbm, vp_hbm)):
            pltpu.make_async_remote_copy(
                src_ref=ref.at[:, head], dst_ref=landed.at[z, i], send_sem=a_send, recv_sem=a_recv.at[z // PER],
                device_id=device(x, y, zt, core), device_id_type=MESH,
            ).start()

    for zt in range(EARLY):

        @pl.when(z != zt)
        def _():
            give(zt)

    for zt in range(EARLY):

        @pl.when(late)
        def _():
            signal(late_in, x, y, zt, core)

    @pl.when(core == 1)
    def _():
        for dx, dy in OFFSETS[1:]:
            signal(barrier, (x + dx) % NX, (y + dy) % NY, z, 1)
        for zt in range(NZ):
            far_end = z != zt
            if zt < EARLY:
                far_end &= ~late

            @pl.when(far_end & ~early)
            def _():
                signal(barrier, x, y, zt, 1)

    head = pl.ds(pl.multiple_of(z % ZL * HEAD_WIDTH, HEAD_WIDTH), HEAD_WIDTH)
    for i, ref in enumerate((kp_hbm, vp_hbm)):
        pltpu.make_async_copy(ref.at[:, head], landed.at[z, i], a_recv.at[z // PER]).start()

    for load in loads:
        load.wait()
    lower = lax.broadcasted_iota(jnp.int32, (SLOTS, HEAD_WIDTH), 1) < HEAD_WIDTH // 2
    cs = table[...]
    turned = pltpu.roll(cs, HEAD_WIDTH // 2, 1)
    cosine = jnp.where(lower, cs, turned)
    sine = jnp.where(lower, -turned, cs)

    def rotate(rows):
        rows = rows.astype(jnp.float32)
        return (rows * cosine + pltpu.roll(rows, HEAD_WIDTH // 2, 1) * sine).astype(jnp.bfloat16)

    new_keys = rotate(ck[...].reshape(SLOTS, HEAD_WIDTH))
    new_values = cv[...].reshape(SLOTS, HEAD_WIDTH)
    ones = jnp.ones((SLOTS, HEAD_WIDTH), jnp.bfloat16)
    new_values = jnp.concatenate([new_values, ones], axis=1)
    causal = lax.broadcasted_iota(jnp.int32, (SLOTS, SLOTS), 1) <= lax.broadcasted_iota(
        jnp.int32, (SLOTS, SLOTS), 0
    )

    def own(h):
        rows = rotate(q[h])
        q[h] = rows
        s = lax.dot_general(rows, new_keys, (((1,), (1,)), ((), ())), preferred_element_type=jnp.float32)
        s = jnp.where(causal, s * SCALE2, -jnp.inf)
        m = jnp.max(s, axis=1, keepdims=True)
        p = jnp.exp2(s - m).astype(jnp.bfloat16)
        r = pl.ds(h * SLOTS, SLOTS)
        acc[r, :] = jnp.dot(p, new_values, preferred_element_type=jnp.float32)
        top[r, :] = jnp.broadcast_to(m, (SLOTS, HEAD_WIDTH))

    for h in range(GROUP):
        own(h)

    @pl.when(core == 1)
    def _():
        plane, middle = NX * NY - 1, LATE - EARLY
        others = jnp.where(early, middle, NZ - EARLY - 1)
        pl.semaphore_wait(barrier, plane + others)
        signal(all_in, x, y, z, 0)

    @pl.when(core == 0)
    def _():
        pl.semaphore_wait(all_in, 1)

    for zt in range(EARLY, NZ):
        there = z != zt
        if zt >= LATE:
            there &= ~early

        @pl.when(there)
        def _():
            give(zt)

    def quarter(w):
        own = z // PER
        near = (0, 1, 3, 2)[w]
        far = (own, 5 - own, 0, 1)[w]
        return jnp.where(early, near, jnp.where(z < NZ // 2, (0, 1, 3, 2)[w], far))

    place = x * NY + y
    for w in range(WAVES):
        src = quarter(w)
        arrived = landed.at[pl.ds(src * PER, PER)]
        pltpu.make_async_copy(arrived, arrived, a_recv.at[src]).wait()
        for which in (0, 1):
            rows = [landed[src * PER + i, which].astype(jnp.float32) for i in range(PER)]
            kv[w, core, place, which] = jnp.concatenate(rows, axis=0).astype(jnp.bfloat16)
        def pass_on(tx, ty):
            pltpu.make_async_remote_copy(
                src_ref=kv.at[w, core, place], dst_ref=kv.at[w, core, place], send_sem=p_send.at[w],
                recv_sem=p_recv.at[w], device_id=device(tx, ty, z, core), device_id_type=MESH,
            ).start()
            if w == WAVES - 1:
                pass_across(tx, ty)

        def pass_across(tx, ty):
            @pl.when(core == 0)
            def _():
                pltpu.make_async_remote_copy(
                    src_ref=kv.at[w, 0, place], dst_ref=kv.at[w, 0, place], send_sem=e_send,
                    recv_sem=d_recv.at[w], device_id=device(tx, ty, z, 1), device_id_type=MESH,
                ).start()

        @pl.when(place != 0)
        def _():
            pass_on(0, 0)

        for dx, dy in OFFSETS[1:]:
            tx, ty = (x + dx) % NX, (y + dy) % NY

            @pl.when(tx + ty != 0)
            def _():
                pass_on(tx, ty)

        if w == WAVES - 1:
            pass_across(x, y)

        if w == 1:

            @pl.when(early)
            def _():
                pl.semaphore_wait(late_in, NZ - LATE)
                for zt in range(LATE, NZ):
                    give(zt)

    keys_here = NX * NY * PER * 4
    ones_block = jnp.ones((keys_here, HEAD_WIDTH), jnp.bfloat16)
    mine = (grp * lax.axis_size("seq") + seq) // KEY_VALUE_HEADS

    def attend(w, c, last=False):
        block = kv[w, c]
        keys = block[:, 0].reshape(keys_here, HEAD_WIDTH)
        values = jnp.concatenate([block[:, 1].reshape(keys_here, HEAD_WIDTH), ones_block], axis=1)
        s = lax.dot_general(
            q[...].reshape(ROWS, HEAD_WIDTH), keys, (((1,), (1,)), ((), ())), preferred_element_type=jnp.float32
        )
        tiles = [s[:, t : t + HEAD_WIDTH] for t in range(0, keys_here, HEAD_WIDTH)]
        old = top[...]
        m = jnp.maximum(old, jnp.max(functools.reduce(jnp.maximum, tiles), axis=1, keepdims=True) * SCALE2)
        decline = jnp.exp2(old - m)
        p = jnp.concatenate([jnp.exp2(t * SCALE2 - m).astype(jnp.bfloat16) for t in tiles], axis=1)
        o = acc[...] * jnp.concatenate([decline, decline], axis=1) + jnp.dot(
            p, values, preferred_element_type=jnp.float32
        )
        if not last:
            acc[...] = o
            top[...] = m
        else:
            token = lax.broadcasted_iota(jnp.int32, (ROWS, HEAD_WIDTH), 0) % SLOTS
            result = jnp.where(token < len_ref[mine], o[:, :HEAD_WIDTH] / o[:, HEAD_WIDTH:], 0.0)
            out_ref[...] = result.astype(jnp.bfloat16).reshape(GROUP, SLOTS, HEAD_WIDTH)

    peers = NX * NY - 1
    for w in range(WAVES):
        rest = kv.at[w, core, pl.ds(0, peers)]
        pltpu.make_async_copy(rest, rest, p_recv.at[w]).wait()
        whole = kv.at[w, core]
        if w < WAVES - 1:
            pltpu.make_async_remote_copy(
                src_ref=whole, dst_ref=whole, send_sem=d_send, recv_sem=d_recv.at[w],
                device_id=device(x, y, z, 1 - core), device_id_type=MESH,
            ).start()
        else:

            @pl.when(core == 1)
            def _():
                pltpu.make_async_remote_copy(
                    src_ref=kv.at[w, 1], dst_ref=kv.at[w, 1], send_sem=e_send, recv_sem=d_recv.at[w],
                    device_id=device(x, y, z, 0), device_id_type=MESH,
                ).start()

        if w:
            pltpu.make_async_copy(whole, whole, d_recv.at[w - 1]).wait()
            attend(w - 1, 1 - core)
        attend(w, core)
    pltpu.make_async_copy(whole, whole, d_recv.at[WAVES - 1]).wait()
    attend(WAVES - 1, 1 - core, last=True)

    given = landed.at[pl.ds(0, NZ - 1)]
    pltpu.make_async_copy(given, given, a_send).wait()
    for w in range(WAVES):
        sent = kv.at[w, 0, pl.ds(0, peers)]
        pltpu.make_async_copy(sent, sent, p_send.at[w]).wait()
    before = kv.at[pl.ds(0, WAVES - 1), 0]
    pltpu.make_async_copy(before, before, d_send).wait()
    pltpu.make_async_copy(whole, whole, e_send).wait()


def shards(cand_queries, candidate_keys, candidate_values, prefix_keys, prefix_values, lengths):
    bf16, f32 = jnp.bfloat16, jnp.float32
    anywhere = pl.BlockSpec(memory_space=pl.ANY)
    dma = pltpu.SemaphoreType.DMA
    return pl.pallas_call(
        kernel,
        out_shape=pltpu.VMEM(cand_queries.shape, bf16),
        in_specs=[anywhere] * 6 + [pl.BlockSpec(memory_space=pltpu.SMEM)],
        out_specs=pl.BlockSpec(memory_space=pltpu.VMEM),
        scratch_shapes=[
            pltpu.VMEM(cand_queries.shape, bf16),
            pltpu.VMEM(candidate_keys.shape, bf16),
            pltpu.VMEM(candidate_values.shape, bf16),
            pltpu.VMEM((SLOTS, HEAD_WIDTH), f32),
            pltpu.VMEM((NZ, 2, 4, HEAD_WIDTH), bf16),
            pltpu.VMEM((WAVES, 2, NX * NY, 2, PER * 4, HEAD_WIDTH), bf16),
            pltpu.VMEM((ROWS, 2 * HEAD_WIDTH), f32),
            pltpu.VMEM((ROWS, HEAD_WIDTH), f32),
            dma((4,)),
            dma,
            dma((WAVES,)),
            dma((WAVES,)),
            dma((WAVES,)),
            dma,
            dma((WAVES,)),
            dma,
            pltpu.SemaphoreType.REGULAR,
            pltpu.SemaphoreType.REGULAR,
            pltpu.SemaphoreType.REGULAR,
        ],
        compiler_params=pltpu.CompilerParams(
            collective_id=0, has_side_effects=True, vmem_limit_bytes=60 * 1024 * 1024
        ),
    )(prefix_keys, prefix_values, cand_queries, candidate_keys, candidate_values, jnp.asarray(rotation_table()), lengths)


def solution(mesh):
    split = P(("grp", "seq"), None, None)
    rows = P(("grp", "seq"), None)
    return jax.shard_map(
        shards,
        mesh=mesh,
        in_specs=(split, split, split, rows, rows, P()),
        out_specs=split,
        check_vma=False,
    )
```

```python
import functools
import math

import jax
import jax.numpy as jnp
import numpy as np
from jax import lax
from jax.experimental import pallas as pl
from jax.experimental.pallas import tpu as pltpu
from jax.sharding import PartitionSpec as P

QUERY_HEADS = 64
KEY_VALUE_HEADS = 8
HEAD_WIDTH = 128
SLOTS = 128
PREFIX = 2048
ROPE_BASE = 500000.0
GROUP = QUERY_HEADS // KEY_VALUE_HEADS
ROWS = GROUP * SLOTS
SCALE2 = math.log2(math.e) / math.sqrt(HEAD_WIDTH)

NX, NY, NZ, ZL = 4, 4, 16, 8
MESH = pl.DeviceIdType.MESH
WAVES = 4
EARLY, LATE = 4, 8
PER = NZ // WAVES
OFFSETS = sorted(
    [(dx, dy) for dx in range(NX) for dy in range(NY)],
    key=lambda o: -(min(o[0], NX - o[0]) + min(o[1], NY - o[1])) if any(o) else -99,
)


def rotation_table():
    half = HEAD_WIDTH // 2
    exponents = np.arange(half, dtype=np.float32) * np.float32(2.0 / HEAD_WIDTH)
    frequency = (np.float32(1.0) / np.power(np.float32(ROPE_BASE), exponents)).astype(np.float32)
    positions = np.float32(PREFIX) + np.arange(SLOTS, dtype=np.float32)
    angles = (positions[:, None] * frequency[None, :]).astype(np.float32).astype(np.float64)
    return np.concatenate([np.cos(angles), np.sin(angles)], axis=1).astype(np.float32)


def device(x, y, z, core):
    return ((z // ZL) * 2 + core, (x * NY + y) * ZL + z % ZL)


def kernel(
    kp_hbm, vp_hbm, q_hbm, ck_hbm, cv_hbm, table_hbm, len_ref, out_ref,
    q, ck, cv, table, landed, kv, acc, top,
    in_sem, a_send, a_recv, p_send, p_recv, d_send, d_recv, e_send, ready, late_in, all_in,
):
    grp, seq = lax.axis_index("grp"), lax.axis_index("seq")
    core, zh = grp % 2, grp // 2
    z = zh * ZL + seq % ZL
    y = (seq // ZL) % NY
    x = seq // (ZL * NY)

    loads = [
        pltpu.make_async_copy(s, d, in_sem.at[i])
        for i, (s, d) in enumerate(
            [(q_hbm, q), (ck_hbm, ck), (cv_hbm, cv), (table_hbm, table)]
        )
    ]
    for load in loads:
        load.start()

    barrier = pltpu.get_barrier_semaphore()
    early, late = z < EARLY, z >= LATE

    def signal(sem, *place):
        pl.semaphore_signal(sem, inc=1, device_id=device(*place), device_id_type=MESH)

    for zt in range(NZ):

        @pl.when(early & (z != zt))
        def _():
            signal(barrier, x, y, zt, 0)

    @pl.when(core == 1)
    def _():
        signal(barrier, x, y, z, 0)

    @pl.when(core == 0)
    def _():
        pl.semaphore_wait(barrier, jnp.where(early, 2 * EARLY - 1, 2 * EARLY + 1))
        signal(ready, x, y, z, 1)

    @pl.when(core == 1)
    def _():
        pl.semaphore_wait(ready, 1)

    def give(zt):
        head = pl.ds(zt % ZL * HEAD_WIDTH, HEAD_WIDTH)
        for i, ref in enumerate((kp_hbm, vp_hbm)):
            pltpu.make_async_remote_copy(
                src_ref=ref.at[:, head], dst_ref=landed.at[z, i], send_sem=a_send, recv_sem=a_recv.at[z // PER],
                device_id=device(x, y, zt, core), device_id_type=MESH,
            ).start()

    for zt in range(EARLY):

        @pl.when(z != zt)
        def _():
            give(zt)

    for zt in range(EARLY):

        @pl.when(late)
        def _():
            signal(late_in, x, y, zt, core)

    @pl.when(core == 1)
    def _():
        for dx, dy in OFFSETS[1:]:
            signal(barrier, (x + dx) % NX, (y + dy) % NY, z, 1)
        for zt in range(NZ):
            far_end = z != zt
            if zt < EARLY:
                far_end &= ~late

            @pl.when(far_end & ~early)
            def _():
                signal(barrier, x, y, zt, 1)

    head = pl.ds(pl.multiple_of(z % ZL * HEAD_WIDTH, HEAD_WIDTH), HEAD_WIDTH)
    for i, ref in enumerate((kp_hbm, vp_hbm)):
        pltpu.make_async_copy(ref.at[:, head], landed.at[z, i], a_recv.at[z // PER]).start()

    for load in loads:
        load.wait()
    lower = lax.broadcasted_iota(jnp.int32, (SLOTS, HEAD_WIDTH), 1) < HEAD_WIDTH // 2
    cs = table[...]
    turned = pltpu.roll(cs, HEAD_WIDTH // 2, 1)
    cosine = jnp.where(lower, cs, turned)
    sine = jnp.where(lower, -turned, cs)

    def rotate(rows):
        rows = rows.astype(jnp.float32)
        return (rows * cosine + pltpu.roll(rows, HEAD_WIDTH // 2, 1) * sine).astype(jnp.bfloat16)

    new_keys = rotate(ck[...].reshape(SLOTS, HEAD_WIDTH))
    new_values = cv[...].reshape(SLOTS, HEAD_WIDTH)
    ones = jnp.ones((SLOTS, HEAD_WIDTH), jnp.bfloat16)
    new_values = jnp.concatenate([new_values, ones], axis=1)
    causal = lax.broadcasted_iota(jnp.int32, (SLOTS, SLOTS), 1) <= lax.broadcasted_iota(
        jnp.int32, (SLOTS, SLOTS), 0
    )

    def own(h):
        rows = rotate(q[h])
        q[h] = rows
        s = lax.dot_general(rows, new_keys, (((1,), (1,)), ((), ())), preferred_element_type=jnp.float32)
        s = jnp.where(causal, s * SCALE2, -jnp.inf)
        m = jnp.max(s, axis=1, keepdims=True)
        p = jnp.exp2(s - m).astype(jnp.bfloat16)
        r = pl.ds(h * SLOTS, SLOTS)
        acc[r, :] = jnp.dot(p, new_values, preferred_element_type=jnp.float32)
        top[r, :] = jnp.broadcast_to(m, (SLOTS, HEAD_WIDTH))

    for h in range(GROUP):
        own(h)

    @pl.when(core == 1)
    def _():
        plane, middle = NX * NY - 1, LATE - EARLY
        others = jnp.where(early, middle, NZ - EARLY - 1)
        pl.semaphore_wait(barrier, plane + others)
        signal(all_in, x, y, z, 0)

    @pl.when(core == 0)
    def _():
        pl.semaphore_wait(all_in, 1)

    for zt in range(EARLY, NZ):
        there = z != zt
        if zt >= LATE:
            there &= ~early

        @pl.when(there)
        def _():
            give(zt)

    def quarter(w):
        own = z // PER
        near = (0, 1, 3, 2)[w]
        far = (own, 5 - own, 0, 1)[w]
        return jnp.where(early, near, jnp.where(z < NZ // 2, (0, 1, 2, 3)[w], far))

    place = x * NY + y
    for w in range(WAVES):
        src = quarter(w)
        arrived = landed.at[pl.ds(src * PER, PER)]
        pltpu.make_async_copy(arrived, arrived, a_recv.at[src]).wait()
        for which in (0, 1):
            rows = [landed[src * PER + i, which].astype(jnp.float32) for i in range(PER)]
            kv[w, core, place, which] = jnp.concatenate(rows, axis=0).astype(jnp.bfloat16)
        def pass_on(tx, ty):
            if w == WAVES - 1:
                pass_across(tx, ty)
            pltpu.make_async_remote_copy(
                src_ref=kv.at[w, core, place], dst_ref=kv.at[w, core, place], send_sem=p_send.at[w],
                recv_sem=p_recv.at[w], device_id=device(tx, ty, z, core), device_id_type=MESH,
            ).start()

        def pass_across(tx, ty):
            @pl.when(core == 0)
            def _():
                pltpu.make_async_remote_copy(
                    src_ref=kv.at[w, 0, place], dst_ref=kv.at[w, 0, place], send_sem=e_send,
                    recv_sem=d_recv.at[w], device_id=device(tx, ty, z, 1), device_id_type=MESH,
                ).start()

        @pl.when(place != 0)
        def _():
            pass_on(0, 0)

        for dx, dy in OFFSETS[1:]:
            tx, ty = (x + dx) % NX, (y + dy) % NY

            @pl.when(tx + ty != 0)
            def _():
                pass_on(tx, ty)

        if w == WAVES - 1:
            pass_across(x, y)

        if w == 1:

            @pl.when(early)
            def _():
                pl.semaphore_wait(late_in, NZ - LATE)
                for zt in range(LATE, NZ):
                    give(zt)

    keys_here = NX * NY * PER * 4
    ones_block = jnp.ones((keys_here, HEAD_WIDTH), jnp.bfloat16)
    mine = (grp * lax.axis_size("seq") + seq) // KEY_VALUE_HEADS

    def attend(w, c, last=False):
        block = kv[w, c]
        keys = block[:, 0].reshape(keys_here, HEAD_WIDTH)
        values = jnp.concatenate([block[:, 1].reshape(keys_here, HEAD_WIDTH), ones_block], axis=1)
        s = lax.dot_general(
            q[...].reshape(ROWS, HEAD_WIDTH), keys, (((1,), (1,)), ((), ())), preferred_element_type=jnp.float32
        )
        tiles = [s[:, t : t + HEAD_WIDTH] for t in range(0, keys_here, HEAD_WIDTH)]
        old = top[...]
        m = jnp.maximum(old, jnp.max(functools.reduce(jnp.maximum, tiles), axis=1, keepdims=True) * SCALE2)
        decline = jnp.exp2(old - m)
        p = jnp.concatenate([jnp.exp2(t * SCALE2 - m).astype(jnp.bfloat16) for t in tiles], axis=1)
        o = acc[...] * jnp.concatenate([decline, decline], axis=1) + jnp.dot(
            p, values, preferred_element_type=jnp.float32
        )
        if not last:
            acc[...] = o
            top[...] = m
        else:
            token = lax.broadcasted_iota(jnp.int32, (ROWS, HEAD_WIDTH), 0) % SLOTS
            result = jnp.where(token < len_ref[mine], o[:, :HEAD_WIDTH] / o[:, HEAD_WIDTH:], 0.0)
            out_ref[...] = result.astype(jnp.bfloat16).reshape(GROUP, SLOTS, HEAD_WIDTH)

    peers = NX * NY - 1
    for w in range(WAVES):
        rest = kv.at[w, core, pl.ds(0, peers)]
        pltpu.make_async_copy(rest, rest, p_recv.at[w]).wait()
        whole = kv.at[w, core]
        if w < WAVES - 1:
            pltpu.make_async_remote_copy(
                src_ref=whole, dst_ref=whole, send_sem=d_send, recv_sem=d_recv.at[w],
                device_id=device(x, y, z, 1 - core), device_id_type=MESH,
            ).start()
        else:

            @pl.when(core == 1)
            def _():
                pltpu.make_async_remote_copy(
                    src_ref=kv.at[w, 1], dst_ref=kv.at[w, 1], send_sem=e_send, recv_sem=d_recv.at[w],
                    device_id=device(x, y, z, 0), device_id_type=MESH,
                ).start()

        if w:
            pltpu.make_async_copy(whole, whole, d_recv.at[w - 1]).wait()
            attend(w - 1, 1 - core)
        attend(w, core)
    pltpu.make_async_copy(whole, whole, d_recv.at[WAVES - 1]).wait()
    attend(WAVES - 1, 1 - core, last=True)

    given = landed.at[pl.ds(0, NZ - 1)]
    pltpu.make_async_copy(given, given, a_send).wait()
    for w in range(WAVES):
        sent = kv.at[w, 0, pl.ds(0, peers)]
        pltpu.make_async_copy(sent, sent, p_send.at[w]).wait()
    before = kv.at[pl.ds(0, WAVES - 1), 0]
    pltpu.make_async_copy(before, before, d_send).wait()
    pltpu.make_async_copy(whole, whole, e_send).wait()


def shards(cand_queries, candidate_keys, candidate_values, prefix_keys, prefix_values, lengths):
    bf16, f32 = jnp.bfloat16, jnp.float32
    anywhere = pl.BlockSpec(memory_space=pl.ANY)
    dma = pltpu.SemaphoreType.DMA
    return pl.pallas_call(
        kernel,
        out_shape=pltpu.VMEM(cand_queries.shape, bf16),
        in_specs=[anywhere] * 6 + [pl.BlockSpec(memory_space=pltpu.SMEM)],
        out_specs=pl.BlockSpec(memory_space=pltpu.VMEM),
        scratch_shapes=[
            pltpu.VMEM(cand_queries.shape, bf16),
            pltpu.VMEM(candidate_keys.shape, bf16),
            pltpu.VMEM(candidate_values.shape, bf16),
            pltpu.VMEM((SLOTS, HEAD_WIDTH), f32),
            pltpu.VMEM((NZ, 2, 4, HEAD_WIDTH), bf16),
            pltpu.VMEM((WAVES, 2, NX * NY, 2, PER * 4, HEAD_WIDTH), bf16),
            pltpu.VMEM((ROWS, 2 * HEAD_WIDTH), f32),
            pltpu.VMEM((ROWS, HEAD_WIDTH), f32),
            dma((4,)),
            dma,
            dma((WAVES,)),
            dma((WAVES,)),
            dma((WAVES,)),
            dma,
            dma((WAVES,)),
            dma,
            pltpu.SemaphoreType.REGULAR,
            pltpu.SemaphoreType.REGULAR,
            pltpu.SemaphoreType.REGULAR,
        ],
        compiler_params=pltpu.CompilerParams(
            collective_id=0, has_side_effects=True, vmem_limit_bytes=60 * 1024 * 1024
        ),
    )(prefix_keys, prefix_values, cand_queries, candidate_keys, candidate_values, jnp.asarray(rotation_table()), lengths)


def solution(mesh):
    split = P(("grp", "seq"), None, None)
    rows = P(("grp", "seq"), None)
    return jax.shard_map(
        shards,
        mesh=mesh,
        in_specs=(split, split, split, rows, rows, P()),
        out_specs=split,
        check_vma=False,
    )
```
